32 devices in a mesh: section: 2 (over x), fsdp: 16 (over z, y, core).
Axes of the slice: x: 2, y: 2, z: 4, core: 2. Of those that a mesh axis runs over, the one named last changes fastest.
Arguments:
- inputs: bfloat16 [2, 4096, 8192], P('section', 'fsdp'), may hold values from -6 to 6
- out_grad: bfloat16 [2, 4096, 512], P('section', 'fsdp'), may hold values from -6 to 6
- gain: float32 [2, 8192], P('section'), may hold values from 0.1 to 1.9
- tiles: bfloat16 [2, 192, 128, 128], P('section', 'fsdp'), may hold values from -1 to 1
- tile_rows: int32 [2, 192], P('section', 'fsdp'), may hold values from -1 to 63, as said below
- tile_cols: int32 [2, 192], P('section', 'fsdp'), may hold values from -1 to 3, as said below
Outputs:
- weight_grad: float32 [2, 192, 128, 128], P('section', 'fsdp')
- gain_grad: float32 [2, 8192], P('section', 'fsdp')
- upstream_grad: bfloat16 [2, 4096, 8192], P('section', 'fsdp')
The draws below stay inside these ranges and needn't reach their ends.
Inputs may be any that keep to these rules, and one draw needn't show every extreme that they name: `tile_rows`: in each section the lists name 128 distinct blocks, one per used slot; an unused slot holds -1 in both lists. The 12 slots of one fsdp index hold its blocks first; in every draw half of the fsdp indices hold 12 blocks and the others a third as many. `tile_cols`: column blocks of the slots named in tile_rows; -1 exactly where tile_rows is -1.
All inputs are finite; a program needn't handle non-finite values.
Results may differ from the reference program's by a relative error of at most 0.0029.
Values may be sent and summed in bfloat16 or wider, within the bound.
A program may use at most 192 MiB of HBM per device.

```python
import math
import jax
import jax.numpy as jnp
from jax import lax

D = 8192
KVH = 4
HEAD = 128
TILE = 128
SECTIONS = 2
TOKENS = 4096
KEPT = 128
CAP = 12
SLOTS = 192


def block_lists(key):
    row_blocks = D // TILE
    col_blocks = KVH * HEAD // TILE
    owners = SLOTS // CAP
    average = KEPT // owners

    def one_section(section_key):
        first_key, second_key = jax.random.split(section_key)
        kept_ids = jax.random.permutation(first_key, row_blocks * col_blocks)[:KEPT]
        ranking = jax.random.permutation(second_key, owners)
        counts = jnp.where(ranking < owners // 2, 3 * (average // 2), average // 2)
        offsets = jnp.cumsum(counts) - counts
        slot_ids = jnp.arange(SLOTS)
        owner_of = slot_ids // CAP
        position = slot_ids % CAP
        used = position < counts[owner_of]
        index = jnp.clip(offsets[owner_of] + position, 0, KEPT - 1)
        tile_id = kept_ids[index]
        row_list = jnp.where(used, tile_id // col_blocks, -1).astype(jnp.int32)
        col_list = jnp.where(used, tile_id % col_blocks, -1).astype(jnp.int32)
        return (row_list, col_list)
    section_keys = jax.random.split(key, SECTIONS)
    return jax.vmap(one_section)(section_keys)


def draw_tile_rows(key, part):
    return block_lists(key)[0]


def draw_tile_cols(key, part):
    return block_lists(key)[1]


def draw_out_grad(key, part):
    key = jax.random.fold_in(key, 7)
    width = KVH * HEAD
    ramp = 1.0 + 2.0 * jnp.arange(TOKENS, dtype=jnp.float32) / max(TOKENS - 1, 1)
    first_key = jax.random.fold_in(key, 0)
    base = jnp.clip(jax.random.normal(first_key, (SECTIONS, TOKENS, width), jnp.float32), -5.0, 5.0)
    values = 0.25 * base * ramp[None, :, None]
    return values.astype(jnp.bfloat16)


def shard_levels(rng, dims, pieces, low, largest):
    level = 1.0
    for dim, parts in pieces:
        draws = jax.random.uniform(jax.random.fold_in(jax.random.fold_in(rng, 6), dim), (parts,), jnp.float32, low / len(pieces), largest / len(pieces))
        level = level * jnp.repeat(jnp.exp(draws), dims[dim] // parts).reshape((-1,) + (1,) * (len(dims) - 1 - dim))
    return level


def centred(own_key, shape, spread, reach, pieces=(), kind=jnp.bfloat16):
    values = spread * jax.random.normal(own_key, shape, jnp.float32)
    if pieces:
        values = values * shard_levels(own_key, shape, pieces, -0.22, 0.18)
    return jnp.clip(values, -reach, reach).astype(kind)


def setup_inputs(seed: int = 0) -> dict:
    keys = jax.random.split(jax.random.key(seed), 7)
    return {
        "inputs": centred(keys[0], (SECTIONS, TOKENS, D), 1.0, 6.0, ((0, 2), (1, 16))),
        "out_grad": draw_out_grad(jax.random.fold_in(keys[6], 71), 0),
        "gain": jnp.clip(1.0 + 0.18 * jax.random.normal(keys[2], (SECTIONS, D), jnp.float32), 0.1, 1.9),
        "tiles": centred(keys[3], (SECTIONS, SLOTS, TILE, TILE), 0.0625, 1.0, ((0, 2), (1, 16))),
        "tile_rows": draw_tile_rows(jax.random.fold_in(keys[6], 71), 0),
        "tile_cols": draw_tile_cols(jax.random.fold_in(keys[6], 71), 0),
    }


EPS = 1e-05

def section_backward(inputs_section, grad_section, gain_section, tiles_section, rows_section, cols_section):
    row_blocks = D // TILE
    col_blocks = KVH * HEAD // TILE
    valid = rows_section >= 0
    row_safe = jnp.where(valid, rows_section, 0).astype(jnp.int32)
    col_safe = jnp.where(valid, cols_section, 0).astype(jnp.int32)
    masked = tiles_section.astype(jnp.float32) * valid[:, None, None].astype(jnp.float32)
    blocked = jnp.zeros((row_blocks, col_blocks, TILE, TILE), jnp.float32).at[row_safe, col_safe].add(masked)
    dense = blocked.transpose(0, 2, 1, 3).reshape(D, col_blocks * TILE)
    width = math.gcd(TOKENS, 512)
    input_blocks = inputs_section.reshape(TOKENS // width, width, D)
    grad_blocks = grad_section.reshape(TOKENS // width, width, col_blocks * TILE)

    def step(carry, pair):
        weight_sum, gain_sum = carry
        input_block, grad_block = pair
        wide = input_block.astype(jnp.float32)
        rstd = lax.rsqrt(lax.optimization_barrier(jnp.mean(wide * wide, axis=-1, keepdims=True)) + EPS)
        normed = wide * rstd
        scaled = lax.optimization_barrier((normed * gain_section).astype(jnp.bfloat16)).astype(jnp.float32)
        grad_wide = grad_block.astype(jnp.float32)
        weight_sum = weight_sum + jnp.dot(scaled.T, grad_wide, precision=lax.Precision.HIGHEST)
        feature_grad = jnp.dot(grad_wide, dense.T, precision=lax.Precision.HIGHEST)
        gain_sum = gain_sum + lax.optimization_barrier(jnp.sum(feature_grad * normed, axis=0))
        gained = feature_grad * gain_section
        input_grad = rstd * (gained - normed * lax.optimization_barrier(jnp.mean(gained * normed, axis=-1, keepdims=True)))
        return ((weight_sum, gain_sum), input_grad.astype(jnp.bfloat16))
    init = (jnp.zeros((D, col_blocks * TILE), jnp.float32), jnp.zeros((D,), jnp.float32))
    (weight_sum, gain_sum), input_grads = lax.scan(step, init, (input_blocks, grad_blocks))
    weight_tiles = weight_sum.reshape(row_blocks, TILE, col_blocks, TILE).transpose(0, 2, 1, 3)[row_safe, col_safe]
    weight_tiles = weight_tiles * valid[:, None, None].astype(jnp.float32)
    return (weight_tiles, gain_sum, input_grads.reshape(TOKENS, D))

def reference(inputs, out_grad, gain, tiles, tile_rows, tile_cols):
    weight_list = []
    gain_list = []
    input_list = []
    for section_id in range(SECTIONS):
        weight_tiles, gain_sum, input_grad = section_backward(inputs[section_id], out_grad[section_id], gain[section_id], tiles[section_id], tile_rows[section_id], tile_cols[section_id])
        weight_list.append(weight_tiles)
        gain_list.append(gain_sum)
        input_list.append(input_grad)
    upstream_grad = jnp.roll(jnp.stack(input_list), -1, axis=0)
    return (jnp.stack(weight_list), jnp.stack(gain_list), upstream_grad)
```

```python
import functools

import jax
import jax.numpy as jnp
from jax import lax
from jax.experimental import pallas as pl
from jax.experimental.pallas import tpu as pltpu
from jax.sharding import PartitionSpec as P

EPS = 1e-05
WIDE = 512


def weight_kernel(rows, cols, x_ref, grad_ref, gain_ref, out_ref, dense):
    owner = pl.program_id(0)
    slots, side, _ = out_ref.shape
    width = x_ref.shape[1]

    @pl.when(owner == 0)
    def _():
        def squares(step, total):
            wide = x_ref[:, pl.ds(pl.multiple_of(step * WIDE, WIDE), WIDE)].astype(jnp.float32)
            return total + jnp.sum(wide * wide, axis=-1, keepdims=True)

        total = lax.fori_loop(
            0, width // WIDE, squares, jnp.zeros((x_ref.shape[0], 1), jnp.float32)
        )
        rstd = lax.rsqrt(total / width + EPS)

        def step(i, carry):
            here = pl.ds(pl.multiple_of(i * WIDE, WIDE), WIDE)
            scaled = (x_ref[:, here].astype(jnp.float32) * rstd * gain_ref[:, here]).astype(
                jnp.bfloat16
            )
            dense[here, :] = lax.dot_general(
                scaled, grad_ref[...], (((0,), (0,)), ((), ())), preferred_element_type=jnp.float32
            )
            return carry

        lax.fori_loop(0, width // WIDE, step, 0)

    def pick(slot, carry):
        row = rows[owner * slots + slot]
        col = cols[owner * slots + slot]
        at_row = pl.ds(pl.multiple_of(jnp.maximum(row, 0) * side, side), side)
        at_col = pl.ds(pl.multiple_of(jnp.maximum(col, 0) * side, side), side)
        block = dense[at_row, at_col]
        out_ref[slot] = jnp.where(row >= 0, block, jnp.zeros_like(block))
        return carry

    lax.fori_loop(0, slots, pick, 0)


def weight_sums(x, grads, gain, rows, cols, owners, side):
    tokens, width = x.shape
    slots = rows.shape[0] // owners
    keys = grads.shape[1]
    whole = lambda shape: pl.BlockSpec(shape, lambda i, r, c: (0, 0))
    return pl.pallas_call(
        weight_kernel,
        out_shape=jax.ShapeDtypeStruct((owners * slots, side, side), jnp.float32),
        grid_spec=pltpu.PrefetchScalarGridSpec(
            num_scalar_prefetch=2,
            grid=(owners,),
            in_specs=[whole((tokens, width)), whole((tokens, keys)), whole((1, width))],
            out_specs=pl.BlockSpec((slots, side, side), lambda i, r, c: (i, 0, 0)),
            scratch_shapes=[pltpu.VMEM((width, keys), jnp.float32)],
        ),
        compiler_params=pltpu.CompilerParams(vmem_limit_bytes=40 * 2**20),
        cost_estimate=pl.CostEstimate(
            flops=2 * tokens * width * keys, bytes_accessed=18 * 2**20, transcendentals=0
        ),
        name="weight_sums",
    )(rows, cols, x, grads, gain)


def input_kernel(slot_of, x_ref, grad_ref, gain_ref, tiles_ref, out_ref, dense, feature):
    side = tiles_ref.shape[1]
    tokens, width = x_ref.shape
    keys = grad_ref.shape[1]
    col_blocks = keys // side

    @pl.when(pl.program_id(0) == 0)
    def _():
        def build(row, carry):
            at_row = pl.ds(pl.multiple_of(row * side, side), side)
            for col in range(col_blocks):
                slot = slot_of[row * col_blocks + col]
                block = tiles_ref[jnp.maximum(slot, 0)]
                dense[at_row, col * side : (col + 1) * side] = jnp.where(
                    slot >= 0, block, jnp.zeros_like(block)
                )
            return carry

        lax.fori_loop(0, width // side, build, 0)

    def squares(step, total):
        wide = x_ref[:, pl.ds(pl.multiple_of(step * WIDE, WIDE), WIDE)].astype(jnp.float32)
        return total + jnp.sum(wide * wide, axis=-1, keepdims=True)

    zero = jnp.zeros((tokens, 1), jnp.float32)
    rstd = lax.rsqrt(lax.fori_loop(0, width // WIDE, squares, zero) / width + EPS)

    def product(step, total):
        here = pl.ds(pl.multiple_of(step * WIDE, WIDE), WIDE)
        gained = (
            lax.dot_general(
                grad_ref[...],
                dense[here, :],
                (((1,), (1,)), ((), ())),
                preferred_element_type=jnp.float32,
            )
            * gain_ref[:, here]
        )
        feature[:, here] = gained
        normed = x_ref[:, here].astype(jnp.float32) * rstd
        return total + jnp.sum(gained * normed, axis=-1, keepdims=True)

    mean = lax.fori_loop(0, width // WIDE, product, zero) / width

    def finish(step, carry):
        here = pl.ds(pl.multiple_of(step * WIDE, WIDE), WIDE)
        normed = x_ref[:, here].astype(jnp.float32) * rstd
        out_ref[:, here] = (rstd * (feature[:, here] - normed * mean)).astype(out_ref.dtype)
        return carry

    lax.fori_loop(0, width // WIDE, finish, 0)


def input_part(x, grads, gain, tiles, slot_of):
    tokens, width = x.shape
    keys = grads.shape[1]
    block = min(tokens, 64)
    return pl.pallas_call(
        input_kernel,
        out_shape=jax.ShapeDtypeStruct((tokens, width), jnp.bfloat16),
        grid_spec=pltpu.PrefetchScalarGridSpec(
            num_scalar_prefetch=1,
            grid=(tokens // block,),
            in_specs=[
                pl.BlockSpec((block, width), lambda i, s: (i, 0)),
                pl.BlockSpec((block, keys), lambda i, s: (i, 0)),
                pl.BlockSpec((1, width), lambda i, s: (0, 0)),
                pl.BlockSpec(tiles.shape, lambda i, s: (0, 0, 0)),
            ],
            out_specs=pl.BlockSpec((block, width), lambda i, s: (i, 0)),
            scratch_shapes=[
                pltpu.VMEM((width, keys), jnp.bfloat16),
                pltpu.VMEM((block, width), jnp.float32),
            ],
        ),
        compiler_params=pltpu.CompilerParams(vmem_limit_bytes=40 * 2**20),
        cost_estimate=pl.CostEstimate(
            flops=2 * tokens * width * keys, bytes_accessed=10 * 2**20, transcendentals=0
        ),
        name="input_part",
    )(slot_of, x, grads, gain, tiles)


def reduce_to_owners(sums):
    return lax.psum_scatter(sums, "fsdp", scatter_dimension=0, tiled=True)


def on_device(inputs, out_grad, gain, tiles, tile_rows, tile_cols):
    x, grads, own_tiles = inputs[0], out_grad[0], tiles[0]
    tokens, width = x.shape
    side = own_tiles.shape[-1]
    row_blocks, col_blocks = width // side, grads.shape[1] // side
    owners = lax.axis_size("fsdp")
    sections = lax.axis_size("section")
    section, index = lax.axis_index("section"), lax.axis_index("fsdp")
    behind = [(s, (s - 1) % sections) for s in range(sections)]
    shift = lambda value: lax.ppermute(value, "section", behind)

    next_tiles = shift(own_tiles)
    places = lax.all_gather(
        jnp.concatenate([tile_rows, tile_cols]), ("section", "fsdp"), axis=0, tiled=False
    ).reshape(sections, owners, 2, -1)
    next_places = lax.dynamic_index_in_dim(places, (section + 1) % sections, 0, keepdims=False)
    places = lax.dynamic_index_in_dim(places, section, 0, keepdims=False)
    rows, cols = places[:, 0].reshape(-1), places[:, 1].reshape(-1)
    next_ids = jnp.where(
        next_places[:, 0] >= 0, next_places[:, 0] * col_blocks + next_places[:, 1], -1
    ).reshape(-1)
    all_tiles = lax.all_gather(next_tiles, "fsdp", axis=0, tiled=True)
    hit = next_ids[None, :] == jnp.arange(row_blocks * col_blocks, dtype=jnp.int32)[:, None]
    slot_of = jnp.max(
        jnp.where(hit, jnp.arange(next_ids.shape[0], dtype=jnp.int32)[None, :], -1), axis=1
    )

    next_gain = shift(gain)
    next_grads = shift(grads)
    parts = 4 if tokens % 256 == 0 else 1
    step = tokens // parts
    arrived = []
    behind_of = next_tiles
    for part in range(parts):
        piece, _ = lax.optimization_barrier((x[part * step : (part + 1) * step], behind_of))
        got = shift(piece)
        if part % 2 == 1:
            behind_of = got
        arrived.append(got)

    sums = weight_sums(x, grads, gain, rows, cols, owners, side)
    weight_grad = reduce_to_owners(sums)

    along = jnp.sum(weight_grad * own_tiles.astype(jnp.float32), axis=-1)
    along = lax.all_gather(along, "fsdp", axis=0, tiled=True)
    share = row_blocks // owners
    mine = index * share + jnp.arange(share, dtype=jnp.int32)
    gain_share = jnp.sum(
        jnp.where((rows[None, :] == mine[:, None])[:, :, None], along[None], 0.0), axis=1
    ).reshape(-1)
    gain_share = gain_share / lax.dynamic_slice_in_dim(gain[0], index * share * side, share * side)

    upstream = jnp.concatenate(
        [
            input_part(
                got, next_grads[part * step : (part + 1) * step], next_gain, all_tiles, slot_of
            )
            for part, got in enumerate(arrived)
        ]
    )
    return (weight_grad[None], gain_share[None], upstream[None])


def solution(mesh):
    in_specs = (
        P("section", "fsdp", None),
        P("section", "fsdp", None),
        P("section", None),
        P("section", "fsdp", None, None),
        P("section", "fsdp"),
        P("section", "fsdp"),
    )
    out_specs = (P("section", "fsdp", None, None), P("section", "fsdp"), P("section", "fsdp", None))
    return jax.shard_map(
        on_device, mesh=mesh, in_specs=in_specs, out_specs=out_specs, check_vma=False
    )
```

```python
import functools

import jax
import jax.numpy as jnp
from jax import lax
from jax.experimental import pallas as pl
from jax.experimental.pallas import tpu as pltpu
from jax.sharding import PartitionSpec as P

EPS = 1e-05
WIDE = 512


def weight_kernel(rows, cols, x_ref, grad_ref, gain_ref, out_ref, dense):
    owner = pl.program_id(0)
    slots, side, _ = out_ref.shape
    width = x_ref.shape[1]

    @pl.when(owner == 0)
    def _():
        def squares(step, total):
            wide = x_ref[:, pl.ds(pl.multiple_of(step * WIDE, WIDE), WIDE)].astype(jnp.float32)
            return total + jnp.sum(wide * wide, axis=-1, keepdims=True)

        total = lax.fori_loop(
            0, width // WIDE, squares, jnp.zeros((x_ref.shape[0], 1), jnp.float32)
        )
        rstd = lax.rsqrt(total / width + EPS)

        def step(i, carry):
            here = pl.ds(pl.multiple_of(i * WIDE, WIDE), WIDE)
            scaled = (x_ref[:, here].astype(jnp.float32) * rstd * gain_ref[:, here]).astype(
                jnp.bfloat16
            )
            dense[here, :] = lax.dot_general(
                scaled, grad_ref[...], (((0,), (0,)), ((), ())), preferred_element_type=jnp.float32
            )
            return carry

        lax.fori_loop(0, width // WIDE, step, 0)

    def pick(slot, carry):
        row = rows[owner * slots + slot]
        col = cols[owner * slots + slot]
        at_row = pl.ds(pl.multiple_of(jnp.maximum(row, 0) * side, side), side)
        at_col = pl.ds(pl.multiple_of(jnp.maximum(col, 0) * side, side), side)
        block = dense[at_row, at_col]
        out_ref[slot] = jnp.where(row >= 0, block, jnp.zeros_like(block))
        return carry

    lax.fori_loop(0, slots, pick, 0)


def weight_sums(x, grads, gain, rows, cols, owners, side):
    tokens, width = x.shape
    slots = rows.shape[0] // owners
    keys = grads.shape[1]
    whole = lambda shape: pl.BlockSpec(shape, lambda i, r, c: (0, 0))
    return pl.pallas_call(
        weight_kernel,
        out_shape=jax.ShapeDtypeStruct((owners * slots, side, side), jnp.float32),
        grid_spec=pltpu.PrefetchScalarGridSpec(
            num_scalar_prefetch=2,
            grid=(owners,),
            in_specs=[whole((tokens, width)), whole((tokens, keys)), whole((1, width))],
            out_specs=pl.BlockSpec((slots, side, side), lambda i, r, c: (i, 0, 0)),
            scratch_shapes=[pltpu.VMEM((width, keys), jnp.float32)],
        ),
        compiler_params=pltpu.CompilerParams(vmem_limit_bytes=40 * 2**20),
        cost_estimate=pl.CostEstimate(
            flops=2 * tokens * width * keys, bytes_accessed=18 * 2**20, transcendentals=0
        ),
        name="weight_sums",
    )(rows, cols, x, grads, gain)


def dense_kernel(slot_of, tiles_ref, out_ref):
    side = tiles_ref.shape[1]
    first = pl.program_id(0) * (out_ref.shape[0] // side)
    col_blocks = out_ref.shape[1] // side

    def build(row, carry):
        at_row = pl.ds(pl.multiple_of(row * side, side), side)
        for col in range(col_blocks):
            slot = slot_of[(first + row) * col_blocks + col]
            block = tiles_ref[jnp.maximum(slot, 0)]
            out_ref[at_row, col * side : (col + 1) * side] = jnp.where(
                slot >= 0, block, jnp.zeros_like(block)
            )
        return carry

    lax.fori_loop(0, out_ref.shape[0] // side, build, 0)


def dense_weights(tiles, slot_of, width, keys):
    return pl.pallas_call(
        dense_kernel,
        out_shape=jax.ShapeDtypeStruct((width, keys), tiles.dtype),
        grid_spec=pltpu.PrefetchScalarGridSpec(
            num_scalar_prefetch=1,
            grid=(8,),
            in_specs=[pl.BlockSpec(tiles.shape, lambda i, s: (0, 0, 0))],
            out_specs=pl.BlockSpec((width // 8, keys), lambda i, s: (i, 0)),
        ),
        compiler_params=pltpu.CompilerParams(vmem_limit_bytes=40 * 2**20),
        cost_estimate=pl.CostEstimate(flops=0, bytes_accessed=15 * 2**20, transcendentals=0),
        name="dense_weights",
    )(slot_of, tiles)


def input_kernel(x_ref, grad_ref, gain_ref, dense, out_ref, feature):
    tokens, width = x_ref.shape

    def squares(step, total):
        wide = x_ref[:, pl.ds(pl.multiple_of(step * WIDE, WIDE), WIDE)].astype(jnp.float32)
        return total + jnp.sum(wide * wide, axis=-1, keepdims=True)

    zero = jnp.zeros((tokens, 1), jnp.float32)
    rstd = lax.rsqrt(lax.fori_loop(0, width // WIDE, squares, zero) / width + EPS)

    def product(step, total):
        here = pl.ds(pl.multiple_of(step * WIDE, WIDE), WIDE)
        gained = (
            lax.dot_general(
                grad_ref[...],
                dense[here, :],
                (((1,), (1,)), ((), ())),
                preferred_element_type=jnp.float32,
            )
            * gain_ref[:, here]
        )
        feature[:, here] = gained
        normed = x_ref[:, here].astype(jnp.float32) * rstd
        return total + jnp.sum(gained * normed, axis=-1, keepdims=True)

    mean = lax.fori_loop(0, width // WIDE, product, zero) / width

    def finish(step, carry):
        here = pl.ds(pl.multiple_of(step * WIDE, WIDE), WIDE)
        normed = x_ref[:, here].astype(jnp.float32) * rstd
        out_ref[:, here] = (rstd * (feature[:, here] - normed * mean)).astype(out_ref.dtype)
        return carry

    lax.fori_loop(0, width // WIDE, finish, 0)


def input_part(x, grads, gain, dense):
    tokens, width = x.shape
    keys = grads.shape[1]
    block = min(tokens, 64)
    return pl.pallas_call(
        input_kernel,
        out_shape=jax.ShapeDtypeStruct((tokens, width), jnp.bfloat16),
        grid=(tokens // block,),
        in_specs=[
            pl.BlockSpec((block, width), lambda i: (i, 0)),
            pl.BlockSpec((block, keys), lambda i: (i, 0)),
            pl.BlockSpec((1, width), lambda i: (0, 0)),
            pl.BlockSpec(dense.shape, lambda i: (0, 0)),
        ],
        out_specs=pl.BlockSpec((block, width), lambda i: (i, 0)),
        scratch_shapes=[pltpu.VMEM((block, width), jnp.float32)],
        compiler_params=pltpu.CompilerParams(vmem_limit_bytes=40 * 2**20),
        cost_estimate=pl.CostEstimate(
            flops=2 * tokens * width * keys, bytes_accessed=10 * 2**20, transcendentals=0
        ),
        name="input_part",
    )(x, grads, gain, dense)


def owner_kernel(lines, levels, sums, out_ref, half, near, stage, across, up, down, load, sems):
    index = lax.axis_index("fsdp")
    core, line, level = index % 2, (index // 2) % lines, index // (2 * lines)
    place = lambda at_level, at_line, at_core: (at_level * lines + at_line) * 2 + at_core
    near_send, near_recv, across_send, across_recv, up_send, up_recv, down_send, down_recv = sems

    def copy(source, target, send, recv, device):
        return pltpu.make_async_remote_copy(
            src_ref=source,
            dst_ref=target,
            send_sem=send,
            recv_sem=recv,
            device_id={"fsdp": device},
            device_id_type=pl.DeviceIdType.MESH,
        )

    barrier = pltpu.get_barrier_semaphore()
    greet = lambda device: pl.semaphore_signal(
        barrier, inc=1, device_id={"fsdp": device}, device_id_type=pl.DeviceIdType.MESH
    )
    greet(place(level, line, 1 - core))
    for ahead in range(1, lines):
        greet(place(level, (line + ahead) % lines, core))
    pl.when(level > 0)(lambda: greet(place(level - 1, line, core)))
    pl.when(level < levels - 1)(lambda: greet(place(level + 1, line, core)))
    below = (level + levels - 1) // levels
    above = (2 * (levels - 1) - level) // levels
    pl.semaphore_wait(barrier, lines + below + above)

    middle = levels // 2
    upper = level // middle
    order = []
    for k in range(levels):
        low = levels - 1 - k if k < middle else k - middle
        high = k if k < middle else levels - 1 - k + middle
        order.append((1 - upper) * low + upper * high)

    def to_core(t, y):
        return copy(
            sums.at[place(t, y, 1 - core)],
            near.at[t, y],
            near_send.at[t, y],
            near_recv.at[t, y],
            place(level, line, 1 - core),
        )

    def own(t, y):
        return pltpu.make_async_copy(sums.at[place(t, y, core)], half.at[t, y], load.at[t, y])

    def to_line(t, ahead):
        return copy(
            stage.at[ahead - 1, t],
            across.at[ahead - 1, t],
            across_send.at[ahead - 1, t],
            across_recv.at[ahead - 1, t],
            place(level, (line + ahead) % lines, core),
        )

    def to_up(t):
        return copy(
            half.at[t, line], up.at[t], up_send.at[t], up_recv.at[t], place(level + 1, line, core)
        )

    def to_down(t):
        return copy(
            half.at[t, line],
            down.at[t],
            down_send.at[t],
            down_recv.at[t],
            place(level - 1, line, core),
        )

    for t in order:
        for y in range(lines):
            to_core(t, y).start()
            own(t, y).start()
    for t in order:
        for y in range(lines):
            own(t, y).wait()
            to_core(t, y).wait_recv()
        for ahead in range(1, lines):
            y = (line + ahead) % lines
            stage[ahead - 1, t] = (half[t, y] + near[t, y]).astype(jnp.bfloat16)
            to_line(t, ahead).start()
    for t in order:
        total = half[t, line] + near[t, line]
        for ahead in range(1, lines):
            to_line(t, ahead).wait_recv()
            total = total + across[ahead - 1, t].astype(jnp.float32)
        half[t, line] = total

        @pl.when(level < t)
        def _():
            @pl.when(level > 0)
            def _():
                to_up(t).wait_recv()
                half[t, line] += up[t]

            to_up(t).start()

        @pl.when(level > t)
        def _():
            @pl.when(level < levels - 1)
            def _():
                to_down(t).wait_recv()
                half[t, line] += down[t]

            to_down(t).start()

    out_ref[...] = half[level, line]

    @pl.when(level > 0)
    def _():
        to_up(level).wait_recv()
        out_ref[...] += up[level]

    @pl.when(level < levels - 1)
    def _():
        to_down(level).wait_recv()
        out_ref[...] += down[level]

    for t in order:
        for y in range(lines):
            to_core(t, y).wait_send()
        for ahead in range(1, lines):
            to_line(t, ahead).wait_send()
        pl.when(level < t)(lambda: to_up(t).wait_send())
        pl.when(level > t)(lambda: to_down(t).wait_send())


def reduce_to_owners(sums):
    owners = lax.axis_size("fsdp")
    lines = 2
    while lines * lines * 4 <= owners // 2:
        lines *= 2
    levels = owners // 2 // lines
    slots, side = sums.shape[0] // owners, sums.shape[1]
    block = (slots, side, side)
    dma = lambda *shape: pltpu.SemaphoreType.DMA(shape)
    return pl.pallas_call(
        functools.partial(owner_kernel, lines, levels),
        out_shape=jax.ShapeDtypeStruct(block, jnp.float32),
        in_specs=[pl.BlockSpec(memory_space=pl.ANY)],
        out_specs=pl.BlockSpec(memory_space=pltpu.VMEM),
        scratch_shapes=[
            pltpu.VMEM((levels, lines) + block, jnp.float32),
            pltpu.VMEM((levels, lines) + block, jnp.float32),
            pltpu.VMEM((lines - 1, levels) + block, jnp.bfloat16),
            pltpu.VMEM((lines - 1, levels) + block, jnp.bfloat16),
            pltpu.VMEM((levels,) + block, jnp.float32),
            pltpu.VMEM((levels,) + block, jnp.float32),
            dma(levels, lines),
            [
                dma(levels, lines),
                dma(levels, lines),
                dma(lines - 1, levels),
                dma(lines - 1, levels),
                dma(levels),
                dma(levels),
                dma(levels),
                dma(levels),
            ],
        ],
        compiler_params=pltpu.CompilerParams(
            collective_id=0, has_side_effects=True, vmem_limit_bytes=40 * 2**20
        ),
        cost_estimate=pl.CostEstimate(
            flops=10**7, bytes_accessed=250 * 2**20, transcendentals=0
        ),
        name="owner_sums",
    )(sums.reshape((owners,) + block))


def on_device(inputs, out_grad, gain, tiles, tile_rows, tile_cols):
    x, grads, own_tiles = inputs[0], out_grad[0], tiles[0]
    tokens, width = x.shape
    side = own_tiles.shape[-1]
    row_blocks, col_blocks = width // side, grads.shape[1] // side
    owners = lax.axis_size("fsdp")
    sections = lax.axis_size("section")
    section, index = lax.axis_index("section"), lax.axis_index("fsdp")
    behind = [(s, (s - 1) % sections) for s in range(sections)]
    shift = lambda value: lax.ppermute(value, "section", behind)

    next_tiles = shift(own_tiles)
    places = lax.all_gather(
        jnp.concatenate([tile_rows, tile_cols]), ("section", "fsdp"), axis=0, tiled=False
    ).reshape(sections, owners, 2, -1)
    next_places = lax.dynamic_index_in_dim(places, (section + 1) % sections, 0, keepdims=False)
    places = lax.dynamic_index_in_dim(places, section, 0, keepdims=False)
    rows, cols = places[:, 0].reshape(-1), places[:, 1].reshape(-1)
    next_ids = jnp.where(
        next_places[:, 0] >= 0, next_places[:, 0] * col_blocks + next_places[:, 1], -1
    ).reshape(-1)
    next_tiles, next_ids = lax.optimization_barrier((next_tiles, next_ids))
    all_tiles = lax.all_gather(next_tiles, "fsdp", axis=0, tiled=True)
    hit = next_ids[None, :] == jnp.arange(row_blocks * col_blocks, dtype=jnp.int32)[:, None]
    slot_of = jnp.max(
        jnp.where(hit, jnp.arange(next_ids.shape[0], dtype=jnp.int32)[None, :], -1), axis=1
    )

    next_gain = shift(gain)
    next_grads = shift(grads)
    parts = 4 if tokens % 256 == 0 else 1
    step = tokens // parts
    arrived = []
    x_later, _ = lax.optimization_barrier((x, next_tiles))
    for part in range(parts):
        arrived.append(shift(x_later[part * step : (part + 1) * step]))

    x_first, _ = lax.optimization_barrier((x, next_tiles))
    sums = weight_sums(x_first, grads, gain, rows, cols, owners, side)
    weight_grad = reduce_to_owners(sums)

    along = jnp.sum(weight_grad * own_tiles.astype(jnp.float32), axis=-1)
    along = lax.all_gather(along, "fsdp", axis=0, tiled=True)
    share = row_blocks // owners
    mine = index * share + jnp.arange(share, dtype=jnp.int32)
    gain_share = jnp.sum(
        jnp.where((rows[None, :] == mine[:, None])[:, :, None], along[None], 0.0), axis=1
    ).reshape(-1)
    gain_share = gain_share / lax.dynamic_slice_in_dim(gain[0], index * share * side, share * side)

    dense = dense_weights(all_tiles, slot_of, width, grads.shape[1])
    upstream = jnp.concatenate(
        [
            input_part(got, next_grads[part * step : (part + 1) * step], next_gain, dense)
            for part, got in enumerate(arrived)
        ]
    )
    return (weight_grad[None], gain_share[None], upstream[None])


def solution(mesh):
    in_specs = (
        P("section", "fsdp", None),
        P("section", "fsdp", None),
        P("section", None),
        P("section", "fsdp", None, None),
        P("section", "fsdp"),
        P("section", "fsdp"),
    )
    out_specs = (P("section", "fsdp", None, None), P("section", "fsdp"), P("section", "fsdp", None))
    return jax.shard_map(
        on_device, mesh=mesh, in_specs=in_specs, out_specs=out_specs, check_vma=False
    )
```

```python
import functools

import jax
import jax.numpy as jnp
from jax import lax
from jax.experimental import pallas as pl
from jax.experimental.pallas import tpu as pltpu
from jax.sharding import PartitionSpec as P

EPS = 1e-05
WIDE = 512


def weight_kernel(rows, cols, x_ref, grad_ref, gain_ref, out_ref, dense):
    owner = pl.program_id(0)
    slots, side, _ = out_ref.shape
    width = x_ref.shape[1]

    @pl.when(owner == 0)
    def _():
        def squares(step, total):
            wide = x_ref[:, pl.ds(pl.multiple_of(step * WIDE, WIDE), WIDE)].astype(jnp.float32)
            return total + jnp.sum(wide * wide, axis=-1, keepdims=True)

        total = lax.fori_loop(
            0, width // WIDE, squares, jnp.zeros((x_ref.shape[0], 1), jnp.float32)
        )
        rstd = lax.rsqrt(total / width + EPS)

        def step(i, carry):
            here = pl.ds(pl.multiple_of(i * WIDE, WIDE), WIDE)
            scaled = (x_ref[:, here].astype(jnp.float32) * rstd * gain_ref[:, here]).astype(
                jnp.bfloat16
            )
            dense[here, :] = lax.dot_general(
                scaled, grad_ref[...], (((0,), (0,)), ((), ())), preferred_element_type=jnp.float32
            )
            return carry

        lax.fori_loop(0, width // WIDE, step, 0)

    def pick(slot, carry):
        row = rows[owner * slots + slot]
        col = cols[owner * slots + slot]
        at_row = pl.ds(pl.multiple_of(jnp.maximum(row, 0) * side, side), side)
        at_col = pl.ds(pl.multiple_of(jnp.maximum(col, 0) * side, side), side)
        block = dense[at_row, at_col]
        out_ref[slot] = jnp.where(row >= 0, block, jnp.zeros_like(block))
        return carry

    lax.fori_loop(0, slots, pick, 0)


def weight_sums(x, grads, gain, rows, cols, owners, side):
    tokens, width = x.shape
    slots = rows.shape[0] // owners
    keys = grads.shape[1]
    whole = lambda shape: pl.BlockSpec(shape, lambda i, r, c: (0, 0))
    return pl.pallas_call(
        weight_kernel,
        out_shape=jax.ShapeDtypeStruct((owners * slots, side, side), jnp.float32),
        grid_spec=pltpu.PrefetchScalarGridSpec(
            num_scalar_prefetch=2,
            grid=(owners,),
            in_specs=[whole((tokens, width)), whole((tokens, keys)), whole((1, width))],
            out_specs=pl.BlockSpec((slots, side, side), lambda i, r, c: (i, 0, 0)),
            scratch_shapes=[pltpu.VMEM((width, keys), jnp.float32)],
        ),
        compiler_params=pltpu.CompilerParams(vmem_limit_bytes=40 * 2**20),
        cost_estimate=pl.CostEstimate(
            flops=2 * tokens * width * keys, bytes_accessed=18 * 2**20, transcendentals=0
        ),
        name="weight_sums",
    )(rows, cols, x, grads, gain)


def input_kernel(slot_of, x_ref, grad_ref, gain_ref, tiles_ref, out_ref, dense, feature):
    side = tiles_ref.shape[1]
    tokens, width = x_ref.shape
    keys = grad_ref.shape[1]
    col_blocks = keys // side

    @pl.when(pl.program_id(0) == 0)
    def _():
        def build(row, carry):
            at_row = pl.ds(pl.multiple_of(row * side, side), side)
            for col in range(col_blocks):
                slot = slot_of[row * col_blocks + col]
                block = tiles_ref[jnp.maximum(slot, 0)]
                dense[at_row, col * side : (col + 1) * side] = jnp.where(
                    slot >= 0, block, jnp.zeros_like(block)
                )
            return carry

        lax.fori_loop(0, width // side, build, 0)

    def squares(step, total):
        wide = x_ref[:, pl.ds(pl.multiple_of(step * WIDE, WIDE), WIDE)].astype(jnp.float32)
        return total + jnp.sum(wide * wide, axis=-1, keepdims=True)

    zero = jnp.zeros((tokens, 1), jnp.float32)
    rstd = lax.rsqrt(lax.fori_loop(0, width // WIDE, squares, zero) / width + EPS)

    def product(step, total):
        here = pl.ds(pl.multiple_of(step * WIDE, WIDE), WIDE)
        gained = (
            lax.dot_general(
                grad_ref[...],
                dense[here, :],
                (((1,), (1,)), ((), ())),
                preferred_element_type=jnp.float32,
            )
            * gain_ref[:, here]
        )
        feature[:, here] = gained
        normed = x_ref[:, here].astype(jnp.float32) * rstd
        return total + jnp.sum(gained * normed, axis=-1, keepdims=True)

    mean = lax.fori_loop(0, width // WIDE, product, zero) / width

    def finish(step, carry):
        here = pl.ds(pl.multiple_of(step * WIDE, WIDE), WIDE)
        normed = x_ref[:, here].astype(jnp.float32) * rstd
        out_ref[:, here] = (rstd * (feature[:, here] - normed * mean)).astype(out_ref.dtype)
        return carry

    lax.fori_loop(0, width // WIDE, finish, 0)


def input_part(x, grads, gain, tiles, slot_of):
    tokens, width = x.shape
    keys = grads.shape[1]
    block = min(tokens, 128)
    return pl.pallas_call(
        input_kernel,
        out_shape=jax.ShapeDtypeStruct((tokens, width), jnp.bfloat16),
        grid_spec=pltpu.PrefetchScalarGridSpec(
            num_scalar_prefetch=1,
            grid=(tokens // block,),
            in_specs=[
                pl.BlockSpec((block, width), lambda i, s: (i, 0)),
                pl.BlockSpec((block, keys), lambda i, s: (i, 0)),
                pl.BlockSpec((1, width), lambda i, s: (0, 0)),
                pl.BlockSpec(tiles.shape, lambda i, s: (0, 0, 0)),
            ],
            out_specs=pl.BlockSpec((block, width), lambda i, s: (i, 0)),
            scratch_shapes=[
                pltpu.VMEM((width, keys), jnp.bfloat16),
                pltpu.VMEM((block, width), jnp.float32),
            ],
        ),
        compiler_params=pltpu.CompilerParams(vmem_limit_bytes=40 * 2**20),
        cost_estimate=pl.CostEstimate(
            flops=2 * tokens * width * keys, bytes_accessed=10 * 2**20, transcendentals=0
        ),
        name="input_part",
    )(slot_of, x, grads, gain, tiles)


def share_kernel(owners, value_ref, out_ref, held, send, recv):
    index = lax.axis_index("fsdp")

    def copy(ahead):
        return pltpu.make_async_remote_copy(
            src_ref=value_ref,
            dst_ref=held.at[index],
            send_sem=send.at[ahead - 1],
            recv_sem=recv.at[ahead - 1],
            device_id={"fsdp": (index + ahead) % owners},
            device_id_type=pl.DeviceIdType.MESH,
        )

    barrier = pltpu.get_barrier_semaphore()
    for ahead in range(1, owners):
        pl.semaphore_signal(
            barrier,
            inc=1,
            device_id={"fsdp": (index + ahead) % owners},
            device_id_type=pl.DeviceIdType.MESH,
        )
    pl.semaphore_wait(barrier, owners - 1)
    for ahead in range(1, owners):
        copy(ahead).start()
    held[index] = value_ref[...]
    for ahead in range(1, owners):
        copy(ahead).wait_recv()
    out_ref[...] = held[...]
    for ahead in range(1, owners):
        copy(ahead).wait_send()


def spread(value, collective_id):
    owners = lax.axis_size("fsdp")
    return pl.pallas_call(
        functools.partial(share_kernel, owners),
        out_shape=jax.ShapeDtypeStruct((owners,) + value.shape, value.dtype),
        in_specs=[pl.BlockSpec(memory_space=pltpu.VMEM)],
        out_specs=pl.BlockSpec(memory_space=pltpu.VMEM),
        scratch_shapes=[
            pltpu.VMEM((owners,) + value.shape, value.dtype),
            pltpu.SemaphoreType.DMA((owners - 1,)),
            pltpu.SemaphoreType.DMA((owners - 1,)),
        ],
        compiler_params=pltpu.CompilerParams(collective_id=collective_id, has_side_effects=True),
        cost_estimate=pl.CostEstimate(flops=0, bytes_accessed=10 * 2**20, transcendentals=0),
        name="share_places" if collective_id == 1 else "share_sums",
    )(value)


def owner_kernel(lines, levels, sums, out_ref, half, near, stage, across, up, down, load, sems):
    index = lax.axis_index("fsdp")
    core, line, level = index % 2, (index // 2) % lines, index // (2 * lines)
    place = lambda at_level, at_line, at_core: (at_level * lines + at_line) * 2 + at_core
    near_send, near_recv, across_send, across_recv, up_send, up_recv, down_send, down_recv = sems

    def copy(source, target, send, recv, device):
        return pltpu.make_async_remote_copy(
            src_ref=source,
            dst_ref=target,
            send_sem=send,
            recv_sem=recv,
            device_id={"fsdp": device},
            device_id_type=pl.DeviceIdType.MESH,
        )

    barrier = pltpu.get_barrier_semaphore()
    greet = lambda device: pl.semaphore_signal(
        barrier, inc=1, device_id={"fsdp": device}, device_id_type=pl.DeviceIdType.MESH
    )
    greet(place(level, line, 1 - core))
    for ahead in range(1, lines):
        greet(place(level, (line + ahead) % lines, core))
    pl.when(level > 0)(lambda: greet(place(level - 1, line, core)))
    pl.when(level < levels - 1)(lambda: greet(place(level + 1, line, core)))
    below = (level + levels - 1) // levels
    above = (2 * (levels - 1) - level) // levels
    pl.semaphore_wait(barrier, lines + below + above)

    middle = levels // 2
    upper = level // middle
    order = []
    for k in range(levels):
        low = levels - 1 - k if k < middle else k - middle
        high = k if k < middle else levels - 1 - k + middle
        order.append((1 - upper) * low + upper * high)

    def to_core(t, y):
        return copy(
            sums.at[place(t, y, 1 - core)],
            near.at[t, y],
            near_send.at[t, y],
            near_recv.at[t, y],
            place(level, line, 1 - core),
        )

    def own(t, y):
        return pltpu.make_async_copy(sums.at[place(t, y, core)], half.at[t, y], load.at[t, y])

    def to_line(t, ahead):
        return copy(
            stage.at[ahead - 1, t],
            across.at[ahead - 1, t],
            across_send.at[ahead - 1, t],
            across_recv.at[ahead - 1, t],
            place(level, (line + ahead) % lines, core),
        )

    def to_up(t):
        return copy(
            half.at[t, line], up.at[t], up_send.at[t], up_recv.at[t], place(level + 1, line, core)
        )

    def to_down(t):
        return copy(
            half.at[t, line],
            down.at[t],
            down_send.at[t],
            down_recv.at[t],
            place(level - 1, line, core),
        )

    for t in order:
        for y in range(lines):
            to_core(t, y).start()
            own(t, y).start()
    for t in order:
        for y in range(lines):
            own(t, y).wait()
            to_core(t, y).wait_recv()
        for ahead in range(1, lines):
            y = (line + ahead) % lines
            stage[ahead - 1, t] = (half[t, y] + near[t, y]).astype(jnp.bfloat16)
            to_line(t, ahead).start()
    for t in order:
        total = half[t, line] + near[t, line]
        for ahead in range(1, lines):
            to_line(t, ahead).wait_recv()
            total = total + across[ahead - 1, t].astype(jnp.float32)
        half[t, line] = total

        @pl.when(level < t)
        def _():
            @pl.when(level > 0)
            def _():
                to_up(t).wait_recv()
                half[t, line] += up[t]

            to_up(t).start()

        @pl.when(level > t)
        def _():
            @pl.when(level < levels - 1)
            def _():
                to_down(t).wait_recv()
                half[t, line] += down[t]

            to_down(t).start()

    out_ref[...] = half[level, line]

    @pl.when(level > 0)
    def _():
        to_up(level).wait_recv()
        out_ref[...] += up[level]

    @pl.when(level < levels - 1)
    def _():
        to_down(level).wait_recv()
        out_ref[...] += down[level]

    for t in order:
        for y in range(lines):
            to_core(t, y).wait_send()
        for ahead in range(1, lines):
            to_line(t, ahead).wait_send()
        pl.when(level < t)(lambda: to_up(t).wait_send())
        pl.when(level > t)(lambda: to_down(t).wait_send())


def reduce_to_owners(sums):
    owners = lax.axis_size("fsdp")
    lines = 2
    while lines * lines * 4 <= owners // 2:
        lines *= 2
    levels = owners // 2 // lines
    slots, side = sums.shape[0] // owners, sums.shape[1]
    block = (slots, side, side)
    dma = lambda *shape: pltpu.SemaphoreType.DMA(shape)
    return pl.pallas_call(
        functools.partial(owner_kernel, lines, levels),
        out_shape=jax.ShapeDtypeStruct(block, jnp.float32),
        in_specs=[pl.BlockSpec(memory_space=pl.ANY)],
        out_specs=pl.BlockSpec(memory_space=pltpu.VMEM),
        scratch_shapes=[
            pltpu.VMEM((levels, lines) + block, jnp.float32),
            pltpu.VMEM((levels, lines) + block, jnp.float32),
            pltpu.VMEM((lines - 1, levels) + block, jnp.bfloat16),
            pltpu.VMEM((lines - 1, levels) + block, jnp.bfloat16),
            pltpu.VMEM((levels,) + block, jnp.float32),
            pltpu.VMEM((levels,) + block, jnp.float32),
            dma(levels, lines),
            [
                dma(levels, lines),
                dma(levels, lines),
                dma(lines - 1, levels),
                dma(lines - 1, levels),
                dma(levels),
                dma(levels),
                dma(levels),
                dma(levels),
            ],
        ],
        compiler_params=pltpu.CompilerParams(
            collective_id=0, has_side_effects=True, vmem_limit_bytes=40 * 2**20
        ),
        cost_estimate=pl.CostEstimate(
            flops=10**7, bytes_accessed=250 * 2**20, transcendentals=0
        ),
        name="owner_sums",
    )(sums.reshape((owners,) + block))


def on_device(inputs, out_grad, gain, tiles, tile_rows, tile_cols):
    x, grads, own_tiles = inputs[0], out_grad[0], tiles[0]
    tokens, width = x.shape
    side = own_tiles.shape[-1]
    row_blocks, col_blocks = width // side, grads.shape[1] // side
    owners = lax.axis_size("fsdp")
    sections = lax.axis_size("section")
    section, index = lax.axis_index("section"), lax.axis_index("fsdp")
    behind = [(s, (s - 1) % sections) for s in range(sections)]
    shift = lambda value: lax.ppermute(value, "section", behind)

    next_tiles = shift(own_tiles)
    slots = tile_rows.shape[1]
    listed = jnp.concatenate([tile_rows, tile_cols])
    places = spread(jnp.pad(listed, ((0, 6), (0, 128 - slots))), 1)[:, :2, :slots]
    next_places = shift(places)
    rows, cols = places[:, 0].reshape(-1), places[:, 1].reshape(-1)
    next_ids = jnp.where(
        next_places[:, 0] >= 0, next_places[:, 0] * col_blocks + next_places[:, 1], -1
    ).reshape(-1)
    next_tiles, places = lax.optimization_barrier((next_tiles, places))
    all_tiles = lax.all_gather(next_tiles, "fsdp", axis=0, tiled=True)
    hit = next_ids[None, :] == jnp.arange(row_blocks * col_blocks, dtype=jnp.int32)[:, None]
    slot_of = jnp.max(
        jnp.where(hit, jnp.arange(next_ids.shape[0], dtype=jnp.int32)[None, :], -1), axis=1
    )

    next_gain = shift(gain)
    next_grads = shift(grads)
    x_later, _ = lax.optimization_barrier((x, next_tiles))
    arrived = shift(x_later)

    x_first, _ = lax.optimization_barrier((x, next_tiles))
    sums = weight_sums(x_first, grads, gain, rows, cols, owners, side)
    weight_grad = reduce_to_owners(sums)

    along = jnp.sum(weight_grad * own_tiles.astype(jnp.float32), axis=-1)
    along = spread(jnp.pad(along, ((0, -slots % 8), (0, 0))), 2)[:, :slots].reshape(-1, side)
    share = row_blocks // owners
    mine = index * share + jnp.arange(share, dtype=jnp.int32)
    gain_share = jnp.sum(
        jnp.where((rows[None, :] == mine[:, None])[:, :, None], along[None], 0.0), axis=1
    ).reshape(-1)
    gain_share = gain_share / lax.dynamic_slice_in_dim(gain[0], index * share * side, share * side)

    upstream = input_part(arrived, next_grads, next_gain, all_tiles, slot_of)
    return (weight_grad[None], gain_share[None], upstream[None])


def solution(mesh):
    in_specs = (
        P("section", "fsdp", None),
        P("section", "fsdp", None),
        P("section", None),
        P("section", "fsdp", None, None),
        P("section", "fsdp"),
        P("section", "fsdp"),
    )
    out_specs = (P("section", "fsdp", None, None), P("section", "fsdp"), P("section", "fsdp", None))
    return jax.shard_map(
        on_device, mesh=mesh, in_specs=in_specs, out_specs=out_specs, check_vma=False
    )
```

```python
import functools

import jax
import jax.numpy as jnp
from jax import lax
from jax.experimental import pallas as pl
from jax.experimental.pallas import tpu as pltpu
from jax.sharding import PartitionSpec as P

EPS = 1e-05
WIDE = 512


def weight_kernel(rows, cols, x_ref, grad_ref, gain_ref, out_ref, dense):
    owner = pl.program_id(0)
    slots, side, _ = out_ref.shape
    width = x_ref.shape[1]

    @pl.when(owner == 0)
    def _():
        def squares(step, total):
            wide = x_ref[:, pl.ds(pl.multiple_of(step * WIDE, WIDE), WIDE)].astype(jnp.float32)
            return total + jnp.sum(wide * wide, axis=-1, keepdims=True)

        total = lax.fori_loop(
            0, width // WIDE, squares, jnp.zeros((x_ref.shape[0], 1), jnp.float32)
        )
        rstd = lax.rsqrt(total / width + EPS)

        def step(i, carry):
            here = pl.ds(pl.multiple_of(i * WIDE, WIDE), WIDE)
            scaled = (x_ref[:, here].astype(jnp.float32) * rstd * gain_ref[:, here]).astype(
                jnp.bfloat16
            )
            dense[here, :] = lax.dot_general(
                scaled, grad_ref[...], (((0,), (0,)), ((), ())), preferred_element_type=jnp.float32
            )
            return carry

        lax.fori_loop(0, width // WIDE, step, 0)

    def pick(slot, carry):
        row = rows[owner * slots + slot]
        col = cols[owner * slots + slot]
        at_row = pl.ds(pl.multiple_of(jnp.maximum(row, 0) * side, side), side)
        at_col = pl.ds(pl.multiple_of(jnp.maximum(col, 0) * side, side), side)
        block = dense[at_row, at_col]
        out_ref[slot] = jnp.where(row >= 0, block, jnp.zeros_like(block))
        return carry

    lax.fori_loop(0, slots, pick, 0)


def weight_sums(x, grads, gain, rows, cols, owners, side):
    tokens, width = x.shape
    slots = rows.shape[0] // owners
    keys = grads.shape[1]
    whole = lambda shape: pl.BlockSpec(shape, lambda i, r, c: (0, 0))
    return pl.pallas_call(
        weight_kernel,
        out_shape=jax.ShapeDtypeStruct((owners * slots, side, side), jnp.float32),
        grid_spec=pltpu.PrefetchScalarGridSpec(
            num_scalar_prefetch=2,
            grid=(owners,),
            in_specs=[whole((tokens, width)), whole((tokens, keys)), whole((1, width))],
            out_specs=pl.BlockSpec((slots, side, side), lambda i, r, c: (i, 0, 0)),
            scratch_shapes=[pltpu.VMEM((width, keys), jnp.float32)],
        ),
        compiler_params=pltpu.CompilerParams(vmem_limit_bytes=40 * 2**20),
        cost_estimate=pl.CostEstimate(
            flops=2 * tokens * width * keys, bytes_accessed=18 * 2**20, transcendentals=0
        ),
        name="weight_sums",
    )(rows, cols, x, grads, gain)


def input_kernel(slot_of, x_ref, grad_ref, gain_ref, tiles_ref, out_ref, dense, feature):
    side = tiles_ref.shape[1]
    tokens, width = x_ref.shape
    keys = grad_ref.shape[1]
    col_blocks = keys // side

    @pl.when(pl.program_id(0) == 0)
    def _():
        def build(row, carry):
            at_row = pl.ds(pl.multiple_of(row * side, side), side)
            for col in range(col_blocks):
                slot = slot_of[row * col_blocks + col]
                block = tiles_ref[jnp.maximum(slot, 0)]
                dense[at_row, col * side : (col + 1) * side] = jnp.where(
                    slot >= 0, block, jnp.zeros_like(block)
                )
            return carry

        lax.fori_loop(0, width // side, build, 0)

    def squares(step, total):
        wide = x_ref[:, pl.ds(pl.multiple_of(step * WIDE, WIDE), WIDE)].astype(jnp.float32)
        return total + jnp.sum(wide * wide, axis=-1, keepdims=True)

    zero = jnp.zeros((tokens, 1), jnp.float32)
    rstd = lax.rsqrt(lax.fori_loop(0, width // WIDE, squares, zero) / width + EPS)

    def product(step, total):
        here = pl.ds(pl.multiple_of(step * WIDE, WIDE), WIDE)
        gained = (
            lax.dot_general(
                grad_ref[...],
                dense[here, :],
                (((1,), (1,)), ((), ())),
                preferred_element_type=jnp.float32,
            )
            * gain_ref[:, here]
        )
        feature[:, here] = gained
        normed = x_ref[:, here].astype(jnp.float32) * rstd
        return total + jnp.sum(gained * normed, axis=-1, keepdims=True)

    mean = lax.fori_loop(0, width // WIDE, product, zero) / width

    def finish(step, carry):
        here = pl.ds(pl.multiple_of(step * WIDE, WIDE), WIDE)
        normed = x_ref[:, here].astype(jnp.float32) * rstd
        out_ref[:, here] = (rstd * (feature[:, here] - normed * mean)).astype(out_ref.dtype)
        return carry

    lax.fori_loop(0, width // WIDE, finish, 0)


def input_part(x, grads, gain, tiles, slot_of):
    tokens, width = x.shape
    keys = grads.shape[1]
    block = min(tokens, 128)
    return pl.pallas_call(
        input_kernel,
        out_shape=jax.ShapeDtypeStruct((tokens, width), jnp.bfloat16),
        grid_spec=pltpu.PrefetchScalarGridSpec(
            num_scalar_prefetch=1,
            grid=(tokens // block,),
            in_specs=[
                pl.BlockSpec((block, width), lambda i, s: (i, 0)),
                pl.BlockSpec((block, keys), lambda i, s: (i, 0)),
                pl.BlockSpec((1, width), lambda i, s: (0, 0)),
                pl.BlockSpec(tiles.shape, lambda i, s: (0, 0, 0)),
            ],
            out_specs=pl.BlockSpec((block, width), lambda i, s: (i, 0)),
            scratch_shapes=[
                pltpu.VMEM((width, keys), jnp.bfloat16),
                pltpu.VMEM((block, width), jnp.float32),
            ],
        ),
        compiler_params=pltpu.CompilerParams(vmem_limit_bytes=40 * 2**20),
        cost_estimate=pl.CostEstimate(
            flops=2 * tokens * width * keys, bytes_accessed=10 * 2**20, transcendentals=0
        ),
        name="input_part",
    )(slot_of, x, grads, gain, tiles)


def share_kernel(owners, value_ref, out_ref, held, send, recv):
    index = lax.axis_index("fsdp")

    def copy(ahead):
        return pltpu.make_async_remote_copy(
            src_ref=value_ref,
            dst_ref=held.at[index],
            send_sem=send.at[ahead - 1],
            recv_sem=recv.at[ahead - 1],
            device_id={"fsdp": (index + ahead) % owners},
            device_id_type=pl.DeviceIdType.MESH,
        )

    barrier = pltpu.get_barrier_semaphore()
    for ahead in range(1, owners):
        pl.semaphore_signal(
            barrier,
            inc=1,
            device_id={"fsdp": (index + ahead) % owners},
            device_id_type=pl.DeviceIdType.MESH,
        )
    pl.semaphore_wait(barrier, owners - 1)
    for ahead in range(1, owners):
        copy(ahead).start()
    held[index] = value_ref[...]
    for ahead in range(1, owners):
        copy(ahead).wait_recv()
    out_ref[...] = held[...]
    for ahead in range(1, owners):
        copy(ahead).wait_send()


def spread(value, collective_id):
    owners = lax.axis_size("fsdp")
    return pl.pallas_call(
        functools.partial(share_kernel, owners),
        out_shape=jax.ShapeDtypeStruct((owners,) + value.shape, value.dtype),
        in_specs=[pl.BlockSpec(memory_space=pltpu.VMEM)],
        out_specs=pl.BlockSpec(memory_space=pltpu.VMEM),
        scratch_shapes=[
            pltpu.VMEM((owners,) + value.shape, value.dtype),
            pltpu.SemaphoreType.DMA((owners - 1,)),
            pltpu.SemaphoreType.DMA((owners - 1,)),
        ],
        compiler_params=pltpu.CompilerParams(collective_id=collective_id, has_side_effects=True),
        cost_estimate=pl.CostEstimate(flops=0, bytes_accessed=10 * 2**20, transcendentals=0),
        name="share_places" if collective_id == 1 else "share_sums",
    )(value)


def owner_kernel(lines, levels, sums, out_ref, half, near, stage, across, up, down, load, sems):
    index = lax.axis_index("fsdp")
    core, line, level = index % 2, (index // 2) % lines, index // (2 * lines)
    place = lambda at_level, at_line, at_core: (at_level * lines + at_line) * 2 + at_core
    near_send, near_recv, across_send, across_recv, up_send, up_recv, down_send, down_recv = sems

    def copy(source, target, send, recv, device):
        return pltpu.make_async_remote_copy(
            src_ref=source,
            dst_ref=target,
            send_sem=send,
            recv_sem=recv,
            device_id={"fsdp": device},
            device_id_type=pl.DeviceIdType.MESH,
        )

    barrier = pltpu.get_barrier_semaphore()
    greet = lambda device: pl.semaphore_signal(
        barrier, inc=1, device_id={"fsdp": device}, device_id_type=pl.DeviceIdType.MESH
    )
    greet(place(level, line, 1 - core))
    for ahead in range(1, lines):
        greet(place(level, (line + ahead) % lines, core))
    pl.when(level > 0)(lambda: greet(place(level - 1, line, core)))
    pl.when(level < levels - 1)(lambda: greet(place(level + 1, line, core)))
    below = (level + levels - 1) // levels
    above = (2 * (levels - 1) - level) // levels
    pl.semaphore_wait(barrier, lines + below + above)

    middle = levels // 2
    upper = level // middle
    order = []
    for k in range(levels):
        low = levels - 1 - k if k < middle else k - middle
        high = k if k < middle else levels - 1 - k + middle
        order.append((1 - upper) * low + upper * high)

    def to_core(t, y):
        return copy(
            sums.at[place(t, y, 1 - core)],
            near.at[t, y],
            near_send.at[t, y],
            near_recv.at[t, y],
            place(level, line, 1 - core),
        )

    def own(t, y):
        return pltpu.make_async_copy(sums.at[place(t, y, core)], half.at[t, y], load.at[t, y])

    def to_line(t, ahead):
        return copy(
            stage.at[ahead - 1, t],
            across.at[ahead - 1, t],
            across_send.at[ahead - 1, t],
            across_recv.at[ahead - 1, t],
            place(level, (line + ahead) % lines, core),
        )

    def to_up(t):
        return copy(
            half.at[t, line], up.at[t], up_send.at[t], up_recv.at[t], place(level + 1, line, core)
        )

    def to_down(t):
        return copy(
            half.at[t, line],
            down.at[t],
            down_send.at[t],
            down_recv.at[t],
            place(level - 1, line, core),
        )

    for t in order:
        for y in range(lines):
            to_core(t, y).start()
            own(t, y).start()
    for t in order:
        for y in range(lines):
            own(t, y).wait()
            to_core(t, y).wait_recv()
        for ahead in range(1, lines):
            y = (line + ahead) % lines
            stage[ahead - 1, t] = (half[t, y] + near[t, y]).astype(jnp.bfloat16)
            to_line(t, ahead).start()
    for t in order:
        total = half[t, line] + near[t, line]
        for ahead in range(1, lines):
            to_line(t, ahead).wait_recv()
            total = total + across[ahead - 1, t].astype(jnp.float32)
        half[t, line] = total

        @pl.when(level < t)
        def _():
            @pl.when(level > 0)
            def _():
                to_up(t).wait_recv()
                half[t, line] += up[t]

            to_up(t).start()

        @pl.when(level > t)
        def _():
            @pl.when(level < levels - 1)
            def _():
                to_down(t).wait_recv()
                half[t, line] += down[t]

            to_down(t).start()

    out_ref[...] = half[level, line]

    @pl.when(level > 0)
    def _():
        to_up(level).wait_recv()
        out_ref[...] += up[level]

    @pl.when(level < levels - 1)
    def _():
        to_down(level).wait_recv()
        out_ref[...] += down[level]

    for t in order:
        for y in range(lines):
            to_core(t, y).wait_send()
        for ahead in range(1, lines):
            to_line(t, ahead).wait_send()
        pl.when(level < t)(lambda: to_up(t).wait_send())
        pl.when(level > t)(lambda: to_down(t).wait_send())


def reduce_to_owners(sums):
    owners = lax.axis_size("fsdp")
    lines = 2
    while lines * lines * 4 <= owners // 2:
        lines *= 2
    levels = owners // 2 // lines
    slots, side = sums.shape[0] // owners, sums.shape[1]
    block = (slots, side, side)
    dma = lambda *shape: pltpu.SemaphoreType.DMA(shape)
    return pl.pallas_call(
        functools.partial(owner_kernel, lines, levels),
        out_shape=jax.ShapeDtypeStruct(block, jnp.float32),
        in_specs=[pl.BlockSpec(memory_space=pl.ANY)],
        out_specs=pl.BlockSpec(memory_space=pltpu.VMEM),
        scratch_shapes=[
            pltpu.VMEM((levels, lines) + block, jnp.float32),
            pltpu.VMEM((levels, lines) + block, jnp.float32),
            pltpu.VMEM((lines - 1, levels) + block, jnp.bfloat16),
            pltpu.VMEM((lines - 1, levels) + block, jnp.bfloat16),
            pltpu.VMEM((levels,) + block, jnp.float32),
            pltpu.VMEM((levels,) + block, jnp.float32),
            dma(levels, lines),
            [
                dma(levels, lines),
                dma(levels, lines),
                dma(lines - 1, levels),
                dma(lines - 1, levels),
                dma(levels),
                dma(levels),
                dma(levels),
                dma(levels),
            ],
        ],
        compiler_params=pltpu.CompilerParams(
            collective_id=0, has_side_effects=True, vmem_limit_bytes=40 * 2**20
        ),
        cost_estimate=pl.CostEstimate(
            flops=10**7, bytes_accessed=250 * 2**20, transcendentals=0
        ),
        name="owner_sums",
    )(sums.reshape((owners,) + block))


def on_device(inputs, out_grad, gain, tiles, tile_rows, tile_cols):
    x, grads, own_tiles = inputs[0], out_grad[0], tiles[0]
    tokens, width = x.shape
    side = own_tiles.shape[-1]
    row_blocks, col_blocks = width // side, grads.shape[1] // side
    owners = lax.axis_size("fsdp")
    sections = lax.axis_size("section")
    section, index = lax.axis_index("section"), lax.axis_index("fsdp")
    behind = [(s, (s - 1) % sections) for s in range(sections)]
    shift = lambda value: lax.ppermute(value, "section", behind)

    next_tiles = shift(own_tiles)
    slots = tile_rows.shape[1]
    listed = jnp.concatenate([tile_rows, tile_cols])
    places = spread(jnp.pad(listed, ((0, 6), (0, 128 - slots))), 1)[:, :2, :slots]
    next_places = shift(places)
    rows, cols = places[:, 0].reshape(-1), places[:, 1].reshape(-1)
    next_ids = jnp.where(
        next_places[:, 0] >= 0, next_places[:, 0] * col_blocks + next_places[:, 1], -1
    ).reshape(-1)
    next_tiles, places = lax.optimization_barrier((next_tiles, places))
    all_tiles = lax.all_gather(next_tiles, "fsdp", axis=0, tiled=True)
    next_gain = shift(gain)
    next_grads = shift(grads)
    x_later, _, next_ids = lax.optimization_barrier((x, next_tiles, next_ids))
    arrived = shift(x_later)

    hit = next_ids[None, :] == jnp.arange(row_blocks * col_blocks, dtype=jnp.int32)[:, None]
    slot_of = jnp.max(
        jnp.where(hit, jnp.arange(next_ids.shape[0], dtype=jnp.int32)[None, :], -1), axis=1
    )

    x_first, _, _ = lax.optimization_barrier((x, next_tiles, next_ids))
    sums = weight_sums(x_first, grads, gain, rows, cols, owners, side)
    weight_grad = reduce_to_owners(sums)

    along = jnp.sum(weight_grad * own_tiles.astype(jnp.float32), axis=-1)
    along = spread(jnp.pad(along, ((0, -slots % 8), (0, 0))), 2)[:, :slots].reshape(-1, side)
    share = row_blocks // owners
    mine = index * share + jnp.arange(share, dtype=jnp.int32)
    gain_share = jnp.sum(
        jnp.where((rows[None, :] == mine[:, None])[:, :, None], along[None], 0.0), axis=1
    ).reshape(-1)
    gain_share = gain_share / lax.dynamic_slice_in_dim(gain[0], index * share * side, share * side)

    upstream = input_part(arrived, next_grads, next_gain, all_tiles, slot_of)
    return (weight_grad[None], gain_share[None], upstream[None])


def solution(mesh):
    in_specs = (
        P("section", "fsdp", None),
        P("section", "fsdp", None),
        P("section", None),
        P("section", "fsdp", None, None),
        P("section", "fsdp"),
        P("section", "fsdp"),
    )
    out_specs = (P("section", "fsdp", None, None), P("section", "fsdp"), P("section", "fsdp", None))
    return jax.shard_map(
        on_device, mesh=mesh, in_specs=in_specs, out_specs=out_specs, check_vma=False
    )
```
